32 devices in a mesh: parts: 2 (over x), ep: 2 (over core), shadow: 8 (over z, y).
Axes of the slice: x: 2, y: 2, z: 4, core: 2. Of those that a mesh axis runs over, the one named last changes fastest.
Arguments:
- hot_root: int32 [4], P('parts'), parts along dimension 0, may hold values from 0 to 7
- res_rows: bfloat16 [24576, 2048], P(('parts', 'ep', 'shadow')), parts along dimension 0, may hold values from -6 to 6
- res_weight: float32 [24576], P(('parts', 'ep', 'shadow')), parts along dimension 0, may hold values from 0.2 to 1
- cold_rows: bfloat16 [2048, 2048], P(('parts', 'ep', 'shadow')), parts along dimension 0, may hold values from -6 to 6
- cold_experts: int32 [2048, 2], P(('parts', 'ep', 'shadow')), parts along dimension 0, may hold values from 0 to 15, all different within a row; in each aligned block of 64 rows (0 to 63, 64 to 127, ...) at most 16 rows name the same one
- cold_weights: float32 [2048, 2], P(('parts', 'ep', 'shadow')), parts along dimension 0, may hold values from 0.2 to 1
- w_gate_up: bfloat16 [16, 2048, 1024], P(('ep', 'shadow')), may hold values from -0.125 to 0.125
- w_down: bfloat16 [16, 512, 2048], P(('ep', 'shadow')), may hold values from -0.25 to 0.25
Outputs:
- hot_out: bfloat16 [24576, 2048], P(('parts', 'ep', 'shadow')), parts along dimension 0
- cold_out: bfloat16 [2048, 2048], P(('parts', 'ep', 'shadow')), parts along dimension 0
The draws below stay inside these ranges and needn't reach their ends.
There are 2 independent parts, one for each index of `parts`. The reference program is written for one: setup_inputs(seed, part) draws one part's arguments, and reference() takes and returns one part's arrays. A program takes and returns all parts, laid end to end along the dimension named above; an argument that names none is the same for every part. Nothing has to cross between parts.
Inputs may be any that keep to these rules, and one draw needn't show every extreme that they name: `cold_experts`: within the rows of one device no expert is named by more than 16 routes, a bound that some block reaches; the 2 experts of a row differ; every expert is named somewhere in a part.
All inputs are finite; a program needn't handle non-finite values.
Results may differ from the reference program's by a relative error of at most 0.0058.
Values may be sent and summed in bfloat16 or wider, within the bound.
No kernel may reach another device: no remote copies, remote signals or barrier semaphores. Data moves between devices by JAX's collectives and lax.ppermute only.
A program may use at most 64 MiB of HBM per device.

```python
import math
import jax
import jax.numpy as jnp
import numpy as np
from jax import lax

D = 2048
FF = 512
RES_DEV = 768
COLD_DEV = 64
TOP = 2
EXPERTS = 16
CAP = 16
RES_TOTAL = 12288
COLD_TOTAL = 1024
N_EP = 2
N_SHADOW = 8


def block_scale(key, dims, cuts, smallest, high):
    gain, own = 1.0, jax.random.fold_in(key, 6)
    for dim, shards_of in cuts:
        heights = jnp.exp(jax.random.uniform(jax.random.fold_in(own, dim), (shards_of,), jnp.float32, smallest / len(cuts), high / len(cuts)))
        gain = gain * jnp.repeat(heights, dims[dim] // shards_of).reshape([-1 if axis == dim else 1 for axis in range(len(dims))])
    return gain


def shared_out(rng, own, number, rows, amount, top, most, lean):
    order = jax.random.permutation(rng, amount)
    crowded, ordinary = shares(amount, rows * top, most, lean, True), shares(amount, rows * top, most, lean, False)
    places = jnp.arange(amount)

    def named(sizes, rotation):
        used = int((sizes > 0).sum())
        fixed = max(1, used // 4)
        shifted = fixed + (places - fixed + rotation * (used - fixed)) % max(1, amount - fixed)
        return jnp.zeros((amount,), jnp.int32).at[order[jnp.where(places < fixed, places, shifted)]].set(jnp.asarray(sizes, jnp.int32))

    sizes = jnp.where(number % 4 == 0, named(crowded, number // 4), named(ordinary, number - number // 4 - 1))
    mixed = jax.random.permutation(jax.random.fold_in(own, 3), amount)
    giver, sink = mixed[0:amount // 2 * 2:2], mixed[1:amount // 2 * 2:2]
    margin = jnp.minimum(sizes[giver] - 1, most - sizes[sink]) // 2
    margin = jnp.where((giver == order[0]) | (sink == order[0]) | (sizes[sink] == 0), 0, jnp.maximum(margin, 0))
    shifted = jax.random.randint(jax.random.fold_in(own, 4), (amount // 2,), 0, 1 << 20) % (margin + 1)
    sizes = sizes.at[giver].add(-shifted).at[sink].add(shifted)
    items = jnp.searchsorted(jnp.cumsum(sizes), jnp.arange(rows * top), side="right").astype(jnp.int32)
    grid = items.reshape(top, rows).T
    grid = grid[jax.random.permutation(jax.random.fold_in(own, 1), rows)]
    rotation = jax.random.randint(jax.random.fold_in(own, 2), (rows, 1), 0, top)
    return jnp.take_along_axis(grid, (jnp.arange(top)[None, :] + rotation) % top, axis=1)


def shares(number_of, total, limit, slope, full):
    loads = [(1 << 20) // math.isqrt(grade ** slope) + 1 for grade in range(1, number_of + 1)]
    largest = limit if full else min(limit, max(-(-total // number_of), total * loads[0] // sum(loads)))
    least = 1 if total - largest >= number_of - 1 else 0
    given, rest = [largest] + [least] * (number_of - 1), total - largest - least * (number_of - 1)
    while rest > 0:
        movable = [i for i in range(1, number_of) if given[i] < largest] or [i for i in range(1, number_of) if given[i] < limit]
        pool, budget = sum([loads[i] for i in movable]), rest
        for i in movable:
            addition = min(limit - given[i], max(1, budget * loads[i] // pool), rest)
            given[i] = given[i] + addition
            rest = rest - addition
    return np.array(given)


def gaussian(key, extent, width, most, cuts=(), kind=jnp.bfloat16):
    drawn = width * jax.random.normal(key, extent, jnp.float32)
    if cuts:
        drawn = drawn * block_scale(key, extent, cuts, -0.22, 0.18)
    return jnp.clip(drawn, -most, most).astype(kind)


def setup_inputs(seed: int = 0, part: int = 0) -> dict:
    arg_keys = jax.random.split(jax.random.key(seed), 9)
    part_splits = jax.random.split(jax.random.fold_in(arg_keys[8], part), 9)
    hot_root = jax.random.randint(part_splits[0], (N_EP,), 0, N_SHADOW).astype(jnp.int32)
    res_rows = gaussian(part_splits[1], (RES_TOTAL, D), 1.0, 6.0, ((0, 16),))
    res_weight = jnp.clip(0.2 + 0.8 * jax.random.uniform(part_splits[2], (RES_TOTAL,), jnp.float32) ** block_scale(part_splits[2], (RES_TOTAL,), ((0, 16),), -0.2, 0.2), 0.2, 1.0)
    cold_rows = gaussian(part_splits[3], (COLD_TOTAL, D), 1.0, 6.0, ((0, 16),))
    cold_experts_keys = jax.random.split(jax.random.fold_in(part_splits[4], 1), COLD_TOTAL // COLD_DEV)
    cold_experts_turns = jax.random.permutation(jax.random.fold_in(part_splits[4], 3), COLD_TOTAL // COLD_DEV)
    cold_experts = jax.vmap(lambda own, number: shared_out(jax.random.fold_in(part_splits[4], 2), own, number, COLD_DEV, EXPERTS, TOP, CAP, 2))(cold_experts_keys, cold_experts_turns).reshape((COLD_TOTAL, TOP))
    cold_weights = jnp.clip(0.2 + 0.8 * jax.random.uniform(part_splits[5], (COLD_TOTAL, TOP), jnp.float32) ** block_scale(part_splits[5], (COLD_TOTAL, TOP), ((0, 16),), -0.2, 0.2), 0.2, 1.0)
    w_gate_up = gaussian(arg_keys[6], (EXPERTS, D, 2 * FF), D ** -0.5, 0.125, ((0, 16),))
    w_down = gaussian(arg_keys[7], (EXPERTS, FF, D), FF ** -0.5, 0.25, ((0, 16),))
    return {"hot_root": hot_root, "res_rows": res_rows, "res_weight": res_weight, "cold_rows": cold_rows, "cold_experts": cold_experts, "cold_weights": cold_weights, "w_gate_up": w_gate_up, "w_down": w_down}


def expert_apply(group_rows, gate_up, down_proj):
    pre_act = jnp.dot(group_rows, gate_up, preferred_element_type=jnp.float32)
    hidden = (jax.nn.silu(pre_act[:, :FF]) * pre_act[:, FF:]).astype(jnp.bfloat16)
    return jnp.dot(hidden, down_proj, preferred_element_type=jnp.float32)


def reference(hot_root, res_rows, res_weight, cold_rows, cold_experts, cold_weights, w_gate_up, w_down):
    devices_all = N_EP * N_SHADOW
    hot_pieces = []
    for group_index in range(N_EP):
        expert_id = group_index * N_SHADOW + hot_root[group_index]
        start_row = group_index * N_SHADOW * RES_DEV
        group_rows = res_rows[start_row:start_row + N_SHADOW * RES_DEV]
        row_weight = res_weight[start_row:start_row + N_SHADOW * RES_DEV]
        expert_out = expert_apply(group_rows, w_gate_up[expert_id], w_down[expert_id])
        hot_pieces.append((expert_out * row_weight[:, None]).astype(jnp.bfloat16))
    hot_out = jnp.concatenate(hot_pieces, axis=0)

    routes = cold_experts.reshape(devices_all, COLD_DEV * TOP)
    onehot = (routes[:, :, None] == jnp.arange(EXPERTS, dtype=jnp.int32)[None, None, :]).astype(jnp.int32)
    route_rank = jnp.sum((jnp.cumsum(onehot, axis=1) - 1) * onehot, axis=2)
    slot_ids = routes * CAP + route_rank
    sources = jnp.repeat(cold_rows, TOP, axis=0).reshape(devices_all, COLD_DEV * TOP, D)

    def fill_buffer(source_rows, slot_list):
        return jnp.zeros((EXPERTS * CAP, D), source_rows.dtype).at[slot_list].set(source_rows)

    buffers = jax.vmap(fill_buffer)(sources, slot_ids)
    by_expert = buffers.reshape(devices_all, EXPERTS, CAP, D).transpose(1, 0, 2, 3).reshape(EXPERTS, devices_all * CAP, D)

    def serve_expert(expert_index):
        expert_out = expert_apply(by_expert[expert_index], w_gate_up[expert_index], w_down[expert_index])
        return expert_out.astype(jnp.bfloat16)

    served = lax.map(serve_expert, jnp.arange(EXPERTS, dtype=jnp.int32))
    returned = served.reshape(EXPERTS, devices_all, CAP, D).transpose(1, 0, 2, 3).reshape(devices_all, EXPERTS * CAP, D)

    def pick_rows(back_rows, slot_list):
        return back_rows[slot_list]

    picked = jax.vmap(pick_rows)(returned, slot_ids).astype(jnp.float32)
    picked = picked * cold_weights.reshape(devices_all, COLD_DEV * TOP)[:, :, None].astype(jnp.float32)
    cold_out = jnp.sum(picked.reshape(devices_all * COLD_DEV, TOP, D), axis=1).astype(jnp.bfloat16)
    return hot_out, cold_out
```

```python
import jax
import jax.numpy as jnp
from jax import lax
from jax.sharding import PartitionSpec as P

LAG = 2
CHUNKS = 16


def ring_order(mesh):
    n = mesh.shape["shadow"]
    axis = mesh.axis_names.index("shadow")
    index = [0] * mesh.devices.ndim
    spots = []
    for s in range(n):
        index[axis] = s
        spots.append(tuple(getattr(mesh.devices[tuple(index)], "coords", (s,))))
    varying = [a for a in range(len(spots[0])) if len({p[a] for p in spots}) > 1]
    if len(varying) == 2:
        sizes = [len({p[a] for p in spots}) for a in varying]
        if 2 in sizes:
            short = varying[sizes.index(2)]
            long = varying[1 - sizes.index(2)]
            low = min(p[short] for p in spots)
            one = sorted((s for s in range(n) if spots[s][short] == low), key=lambda s: spots[s][long])
            two = sorted((s for s in range(n) if spots[s][short] != low), key=lambda s: -spots[s][long])
            return one + two
    return list(range(n))


def swiglu(pre, hidden_units):
    return (jax.nn.silu(pre[:, :hidden_units]) * pre[:, hidden_units:]).astype(jnp.bfloat16)


def ring_broadcast(order, own, root):
    n = len(order)
    chunks = len(own[0])
    place = jnp.array([order.index(s) for s in range(n)], jnp.int32)
    me = lax.axis_index("shadow")
    ahead = (place[me] - place[root]) % n
    hops = (ahead, (n - ahead) % n)
    ways = (
        [(order[i], order[(i + 1) % n]) for i in range(n)],
        [(order[(i + 1) % n], order[i]) for i in range(n)],
    )
    is_root = me == root
    held = [jnp.zeros((chunks, *own[0][0].shape), own[0][0].dtype) for _ in ways]
    came, last = {}, None
    for t in range(chunks + (n - 1) * LAG):
        mine = [own[i][min(t, chunks - 1)] for i in range(2)]
        if t >= LAG:
            got = came.pop(t - LAG)
            if last is not None:
                got, _ = lax.optimization_barrier((got, last))
            mine = [jnp.where(is_root, mine[i], got[i]) for i in range(2)]
        mine = list(lax.optimization_barrier(tuple(mine)))
        last = mine
        for i in range(2):
            at = jnp.clip(t - LAG * hops[i], 0, chunks - 1)
            held[i] = lax.dynamic_update_slice(held[i], mine[i][None], (at, 0, 0))
        if t < chunks + (n - 2) * LAG:
            came[t] = [lax.ppermute(mine[i], "shadow", ways[i]) for i in range(2)]
    return held


def cut(parts, start, size):
    out = []
    for part in parts:
        rows = part.shape[0]
        low, high = max(start, 0), min(start + size, rows)
        if low < high:
            out.append(part[low:high])
        start -= rows
    return out[0] if len(out) == 1 else jnp.concatenate(out, 0)


def body(order, hot_root, res_rows, res_weight, cold_rows, cold_experts, cold_weights, w_gate_up, w_down):
    gate_up, down = w_gate_up[0], w_down[0]
    hidden_units, width = down.shape
    n_owners = lax.axis_size("ep") * lax.axis_size("shadow")
    per_device, fan_out = cold_experts.shape
    capacity = max(2, 2 * per_device * fan_out // n_owners)

    slot = lax.broadcasted_iota(jnp.int32, (per_device, n_owners * capacity), 1)
    named = [cold_experts[:, k : k + 1] == slot // capacity for k in range(fan_out)]
    count = sum(m.astype(jnp.bfloat16) for m in named)
    before = (
        lax.broadcasted_iota(jnp.int32, (per_device, per_device), 0)
        > lax.broadcasted_iota(jnp.int32, (per_device, per_device), 1)
    ).astype(jnp.bfloat16)
    rank = jnp.dot(before, count, preferred_element_type=jnp.float32)
    here = rank == (slot % capacity).astype(jnp.float32)
    chosen = [m & here for m in named]
    placed = sum(m.astype(jnp.bfloat16) for m in chosen)
    outgoing = lax.dot_general(
        placed, cold_rows, (((0,), (0,)), ((), ())), preferred_element_type=jnp.float32
    ).astype(jnp.bfloat16)
    arrived = lax.all_to_all(outgoing, ("ep", "shadow"), 0, 0, tiled=True)
    pre = jnp.dot(arrived, gate_up, preferred_element_type=jnp.float32)
    served = jnp.dot(swiglu(pre, hidden_units), down, preferred_element_type=jnp.float32)
    returned = lax.all_to_all(served.astype(jnp.bfloat16), ("ep", "shadow"), 0, 0, tiled=True)
    scale = sum(jnp.where(chosen[k], cold_weights[:, k : k + 1], 0.0) for k in range(fan_out))
    high = scale.astype(jnp.bfloat16)
    low = (scale - high.astype(jnp.float32)).astype(jnp.bfloat16)
    cold_out = (
        jnp.dot(high, returned, preferred_element_type=jnp.float32)
        + jnp.dot(low, returned, preferred_element_type=jnp.float32)
    ).astype(jnp.bfloat16)

    root = hot_root[lax.axis_index("ep")]
    half, middle = width // 2, gate_up.shape[0] // 2
    lanes = ([gate_up[:middle], down[:, :half]], [gate_up[middle:], down[:, half:]])
    rows = (middle + hidden_units) // CHUNKS
    own = [[cut(lane, c * rows, rows) for c in range(CHUNKS)] for lane in lanes]
    held = [h.reshape(middle + hidden_units, half) for h in ring_broadcast(order, own, root)]
    pre = jnp.dot(res_rows[:, :middle], held[0][:middle], preferred_element_type=jnp.float32) + jnp.dot(
        res_rows[:, middle:], held[1][:middle], preferred_element_type=jnp.float32
    )
    hidden = swiglu(pre, hidden_units)
    hot_out = jnp.concatenate(
        [
            (jnp.dot(hidden, h[middle:], preferred_element_type=jnp.float32) * res_weight[:, None]).astype(jnp.bfloat16)
            for h in held
        ],
        axis=1,
    )
    return hot_out, cold_out


def solution(mesh):
    order = ring_order(mesh)
    rows = P(("parts", "ep", "shadow"), None)
    owners = P(("ep", "shadow"), None, None)
    in_specs = (P("parts"), rows, P(("parts", "ep", "shadow")), rows, rows, rows, owners, owners)
    return jax.shard_map(
        lambda *args: body(order, *args), mesh=mesh, in_specs=in_specs, out_specs=(rows, rows), check_vma=False
    )
```

```python
import functools

import jax
import jax.numpy as jnp
from jax import lax
from jax.experimental import pallas as pl
from jax.experimental.pallas import tpu as pltpu
from jax.sharding import PartitionSpec as P

CHUNKS = 16
BLOCKS = 2


def ring_order(mesh):
    n = mesh.shape["shadow"]
    axis = mesh.axis_names.index("shadow")
    index = [0] * mesh.devices.ndim
    spots = []
    for s in range(n):
        index[axis] = s
        spots.append(tuple(getattr(mesh.devices[tuple(index)], "coords", (s,))))
    varying = [a for a in range(len(spots[0])) if len({p[a] for p in spots}) > 1]
    if len(varying) == 2:
        sizes = [len({p[a] for p in spots}) for a in varying]
        if 2 in sizes:
            short = varying[sizes.index(2)]
            long = varying[1 - sizes.index(2)]
            low = min(p[short] for p in spots)
            one = sorted((s for s in range(n) if spots[s][short] == low), key=lambda s: spots[s][long])
            two = sorted((s for s in range(n) if spots[s][short] != low), key=lambda s: -spots[s][long])
            return one + two
    return list(range(n))


def swiglu(pre, hidden_units):
    return (jax.nn.silu(pre[:, :hidden_units]) * pre[:, hidden_units:]).astype(jnp.bfloat16)


def hot_kernel(n, chunks, lag, hops, x, weight, gate_up, down, *rest):
    came = rest[:-5]
    out, gate_all, down_all, gate_sem, down_sem = rest[-5:]
    middle, half = gate_all.shape[0] // 2, down_all.shape[1] // 2
    rows = (middle + down_all.shape[0]) // chunks

    @pl.when(pl.program_id(0) == 0)
    def _():
        @pl.when(hops[0] == 0)
        def _():
            pltpu.make_async_copy(gate_up, gate_all, gate_sem).start()
            pltpu.make_async_copy(down, down_all, down_sem).start()

        for way in range(2):
            for h in range(1, n):

                @pl.when(hops[way] == h)
                def _(way=way, h=h):
                    for c in range(chunks):
                        source = came[2 * (c + lag * (h - 1)) + way]
                        at = c * rows
                        gate = min(max(middle - at, 0), rows)
                        if gate:
                            target = gate_all.at[pl.ds(way * middle + at, gate), :]
                            pltpu.make_async_copy(source.at[pl.ds(0, gate), :], target, gate_sem).start()
                        if gate < rows:
                            target = down_all.at[pl.ds(at + gate - middle, rows - gate), pl.ds(way * half, half)]
                            pltpu.make_async_copy(source.at[pl.ds(gate, rows - gate), :], target, down_sem).start()

        pltpu.make_async_copy(gate_all, gate_all, gate_sem).wait()

    pre = jnp.dot(x[...], gate_all[...], preferred_element_type=jnp.float32)
    hidden = swiglu(pre, down_all.shape[0])

    @pl.when(pl.program_id(0) == 0)
    def _():
        pltpu.make_async_copy(down_all, down_all, down_sem).wait()

    total = jnp.dot(hidden, down_all[...], preferred_element_type=jnp.float32)
    out[...] = (total * weight[...]).astype(out.dtype)


def hot_expert(n, lag, hops, x, weight, gate_up, down, came):
    tokens, width = x.shape
    block = tokens // BLOCKS
    whole = pl.BlockSpec(memory_space=pl.ANY)
    return pl.pallas_call(
        functools.partial(hot_kernel, n, CHUNKS, lag),
        grid=(BLOCKS,),
        out_shape=jax.ShapeDtypeStruct((tokens, width), jnp.bfloat16),
        in_specs=[
            pl.BlockSpec(memory_space=pltpu.SMEM),
            pl.BlockSpec((block, width), lambda i: (i, 0)),
            pl.BlockSpec((block, 1), lambda i: (i, 0)),
            whole,
            whole,
            *[whole for _ in came],
        ],
        out_specs=pl.BlockSpec((block, width), lambda i: (i, 0)),
        scratch_shapes=[
            pltpu.VMEM(gate_up.shape, gate_up.dtype),
            pltpu.VMEM(down.shape, down.dtype),
            pltpu.SemaphoreType.DMA,
            pltpu.SemaphoreType.DMA,
        ],
        compiler_params=pltpu.CompilerParams(vmem_limit_bytes=60 * 2**20),
        cost_estimate=pl.CostEstimate(
            flops=2 * tokens * (gate_up.size + down.size), bytes_accessed=20 * 2**20, transcendentals=0
        ),
    )(hops, x, weight, gate_up, down, *came)


def cut(parts, start, size):
    out = []
    for part in parts:
        low, high = max(start, 0), min(start + size, part.shape[0])
        if low < high:
            out.append(part[low:high])
        start -= part.shape[0]
    return out[0] if len(out) == 1 else jnp.concatenate(out, 0)


def join(*values):
    return lax.optimization_barrier(values)


def body(order, hot_root, res_rows, res_weight, cold_rows, cold_experts, cold_weights, w_gate_up, w_down):
    gate_up, down = w_gate_up[0], w_down[0]
    hidden_units, width = down.shape
    n = len(order)
    lag = 2 if n < CHUNKS else 1
    n_owners = lax.axis_size("ep") * n
    per_device, fan_out = cold_experts.shape
    capacity = max(2, 2 * per_device * fan_out // n_owners)

    slot = lax.broadcasted_iota(jnp.int32, (per_device, n_owners * capacity), 1)
    named = [cold_experts[:, k : k + 1] == slot // capacity for k in range(fan_out)]
    count = sum(m.astype(jnp.bfloat16) for m in named)
    before = (
        lax.broadcasted_iota(jnp.int32, (per_device, per_device), 0)
        > lax.broadcasted_iota(jnp.int32, (per_device, per_device), 1)
    ).astype(jnp.bfloat16)
    rank = jnp.dot(before, count, preferred_element_type=jnp.float32)
    here = rank == (slot % capacity).astype(jnp.float32)
    chosen = [m & here for m in named]
    placed = sum(m.astype(jnp.bfloat16) for m in chosen)
    outgoing = lax.dot_general(
        placed, cold_rows, (((0,), (0,)), ((), ())), preferred_element_type=jnp.float32
    ).astype(jnp.bfloat16)
    cold = lax.all_to_all(outgoing, ("ep", "shadow"), 0, 0, tiled=True)

    root = hot_root[lax.axis_index("ep")]
    half, middle = width // 2, gate_up.shape[0] // 2
    lanes = ([gate_up[:middle], down[:, :half]], [gate_up[middle:], down[:, half:]])
    rows = (middle + hidden_units) // CHUNKS
    own = [[cut(lane, c * rows, rows) for c in range(CHUNKS)] for lane in lanes]
    place = jnp.array([order.index(s) for s in range(n)], jnp.int32)
    me = lax.axis_index("shadow")
    ahead = (place[me] - place[root]) % n
    hops = jnp.stack([ahead, (n - ahead) % n])
    ways = (
        [(order[i], order[(i + 1) % n]) for i in range(n)],
        [(order[(i + 1) % n], order[i]) for i in range(n)],
    )
    weight = res_weight[:, None]
    steps = CHUNKS + (n - 2) * lag
    came, last = [], None
    for t in range(steps):
        mine = tuple(own[i][t] for i in range(2)) if t < CHUNKS else None
        if t >= lag:
            got = came[t - lag]
            if t == lag + 1:
                got, hops, weight = join(got, hops, weight)
            elif t == steps * 3 // 8:
                got, cold = join(got, cold)
                pre = jnp.dot(cold, gate_up, preferred_element_type=jnp.float32)
                cold = jnp.dot(swiglu(pre, hidden_units), down, preferred_element_type=jnp.float32).astype(jnp.bfloat16)
            elif t == steps * 3 // 8 + 1:
                got, cold = join(got, cold)
                cold = lax.all_to_all(cold, ("ep", "shadow"), 0, 0, tiled=True)
            elif t == steps * 7 // 8:
                got, cold = join(got, cold)
                scale = sum(jnp.where(chosen[k], cold_weights[:, k : k + 1], 0.0) for k in range(fan_out))
                high = lax.reduce_precision(scale, 8, 7)
                low = (scale - high).astype(jnp.bfloat16)
                cold = (
                    jnp.dot(high.astype(jnp.bfloat16), cold, preferred_element_type=jnp.float32)
                    + jnp.dot(low, cold, preferred_element_type=jnp.float32)
                ).astype(jnp.bfloat16)
            got, _ = join(got, last)
            mine = tuple(jnp.where(me == root, m, g) for m, g in zip(mine, got)) if t < CHUNKS else got
        mine = last = join(*mine)
        came.append(tuple(lax.ppermute(mine[i], "shadow", ways[i]) for i in range(2)))
    came, cold = join(came, cold)
    hot_out = hot_expert(n, lag, hops, res_rows, weight, gate_up, down, [c for pair in came for c in pair])
    return hot_out, cold


def solution(mesh):
    order = ring_order(mesh)
    rows = P(("parts", "ep", "shadow"), None)
    owners = P(("ep", "shadow"), None, None)
    in_specs = (P("parts"), rows, P(("parts", "ep", "shadow")), rows, rows, rows, owners, owners)
    return jax.shard_map(
        lambda *args: body(order, *args), mesh=mesh, in_specs=in_specs, out_specs=(rows, rows), check_vma=False
    )
```

```python
import functools

import jax
import jax.numpy as jnp
from jax import lax
from jax.experimental import pallas as pl
from jax.experimental.pallas import tpu as pltpu
from jax.sharding import PartitionSpec as P

ROWS = 96
BLOCKS = 2


def ring_order(mesh):
    n = mesh.shape["shadow"]
    axis = mesh.axis_names.index("shadow")
    index = [0] * mesh.devices.ndim
    spots = []
    for s in range(n):
        index[axis] = s
        spots.append(tuple(getattr(mesh.devices[tuple(index)], "coords", (s,))))
    varying = [a for a in range(len(spots[0])) if len({p[a] for p in spots}) > 1]
    if len(varying) == 2:
        sizes = [len({p[a] for p in spots}) for a in varying]
        if 2 in sizes:
            short = varying[sizes.index(2)]
            long = varying[1 - sizes.index(2)]
            low = min(p[short] for p in spots)
            one = sorted((s for s in range(n) if spots[s][short] == low), key=lambda s: spots[s][long])
            two = sorted((s for s in range(n) if spots[s][short] != low), key=lambda s: -spots[s][long])
            return one + two
    return list(range(n))


def swiglu(pre, hidden_units):
    return (jax.nn.silu(pre[:, :hidden_units]) * pre[:, hidden_units:]).astype(jnp.bfloat16)


def hot_kernel(n, lag, hops, x, weight, gate_up, down, *rest):
    came = rest[:-5]
    out, gate_all, down_all, gate_sems, down_sem = rest[-5:]
    middle, half = gate_all.shape[0] // 2, down_all.shape[1] // 2
    rows = came[0].shape[0]
    starts = starts_of(middle + down_all.shape[0], rows)
    first = pl.program_id(0) == 0

    @pl.when(first)
    def _():
        @pl.when(hops[0] == 0)
        def _():
            for way in range(2):
                part = pl.ds(way * middle, middle)
                pltpu.make_async_copy(gate_up.at[part, :], gate_all.at[part, :], gate_sems.at[way]).start()
            pltpu.make_async_copy(down, down_all, down_sem).start()

        for way in range(2):
            for h in range(1, n):

                @pl.when(hops[way] == h)
                def _(way=way, h=h):
                    for c, at in enumerate(starts):
                        source = came[2 * (c + lag * (h - 1)) + way]
                        low = c * rows - at
                        gate = min(max(middle - at, low), rows)
                        if low < gate:
                            target = gate_all.at[pl.ds(way * middle + at + low, gate - low), :]
                            part = source.at[pl.ds(low, gate - low), :]
                            pltpu.make_async_copy(part, target, gate_sems.at[way]).start()
                        if gate < rows:
                            target = down_all.at[pl.ds(at + gate - middle, rows - gate), pl.ds(way * half, half)]
                            pltpu.make_async_copy(source.at[pl.ds(gate, rows - gate), :], target, down_sem).start()

    pre = 0.0
    for way in range(2):
        part = pl.ds(way * middle, middle)

        @pl.when(first)
        def _(way=way, part=part):
            pltpu.make_async_copy(gate_all.at[part, :], gate_all.at[part, :], gate_sems.at[way]).wait()

        pre += jnp.dot(x[:, part], gate_all[part, :], preferred_element_type=jnp.float32)
    hidden = swiglu(pre, down_all.shape[0])

    @pl.when(first)
    def _():
        pltpu.make_async_copy(down_all, down_all, down_sem).wait()

    total = jnp.dot(hidden, down_all[...], preferred_element_type=jnp.float32)
    out[...] = (total * weight[...]).astype(out.dtype)


def hot_expert(n, lag, hops, x, weight, gate_up, down, came):
    tokens, width = x.shape
    block = tokens // BLOCKS
    whole = pl.BlockSpec(memory_space=pl.ANY)
    return pl.pallas_call(
        functools.partial(hot_kernel, n, lag),
        grid=(BLOCKS,),
        out_shape=jax.ShapeDtypeStruct((tokens, width), jnp.bfloat16),
        in_specs=[
            pl.BlockSpec(memory_space=pltpu.SMEM),
            pl.BlockSpec((block, width), lambda i: (i, 0)),
            pl.BlockSpec((block, 1), lambda i: (i, 0)),
            whole,
            whole,
            *[whole for _ in came],
        ],
        out_specs=pl.BlockSpec((block, width), lambda i: (i, 0)),
        scratch_shapes=[
            pltpu.VMEM(gate_up.shape, gate_up.dtype),
            pltpu.VMEM(down.shape, down.dtype),
            pltpu.SemaphoreType.DMA((2,)),
            pltpu.SemaphoreType.DMA,
        ],
        compiler_params=pltpu.CompilerParams(vmem_limit_bytes=60 * 2**20),
        cost_estimate=pl.CostEstimate(
            flops=2 * tokens * (gate_up.size + down.size), bytes_accessed=20 * 2**20, transcendentals=0
        ),
    )(hops, x, weight, gate_up, down, *came)


def starts_of(total, rows):
    return [min(at, total - rows) for at in range(0, total, rows)]


def cut(parts, start, size):
    out = []
    for part in parts:
        low, high = max(start, 0), min(start + size, part.shape[0])
        if low < high:
            out.append(part[low:high])
        start -= part.shape[0]
    return out[0] if len(out) == 1 else jnp.concatenate(out, 0)


def join(*values):
    return lax.optimization_barrier(values)


def body(order, hot_root, res_rows, res_weight, cold_rows, cold_experts, cold_weights, w_gate_up, w_down):
    gate_up, down = w_gate_up[0], w_down[0]
    hidden_units, width = down.shape
    n = len(order)
    n_owners = lax.axis_size("ep") * n
    per_device, fan_out = cold_experts.shape
    capacity = max(2, 2 * per_device * fan_out // n_owners)

    slot = lax.broadcasted_iota(jnp.int32, (per_device, n_owners * capacity), 1)
    named = [cold_experts[:, k : k + 1] == slot // capacity for k in range(fan_out)]
    count = sum(m.astype(jnp.bfloat16) for m in named)
    before = (
        lax.broadcasted_iota(jnp.int32, (per_device, per_device), 0)
        > lax.broadcasted_iota(jnp.int32, (per_device, per_device), 1)
    ).astype(jnp.bfloat16)
    rank = jnp.dot(before, count, preferred_element_type=jnp.float32)
    here = rank == (slot % capacity).astype(jnp.float32)
    chosen = [m & here for m in named]
    placed = sum(m.astype(jnp.bfloat16) for m in chosen)
    outgoing = lax.dot_general(
        placed, cold_rows, (((0,), (0,)), ((), ())), preferred_element_type=jnp.float32
    ).astype(jnp.bfloat16)
    cold = lax.all_to_all(outgoing, ("ep", "shadow"), 0, 0, tiled=True)

    root = hot_root[lax.axis_index("ep")]
    half, middle = width // 2, gate_up.shape[0] // 2
    lanes = ([gate_up[:middle], down[:, :half]], [gate_up[middle:], down[:, half:]])
    starts = starts_of(middle + hidden_units, ROWS)
    chunks = len(starts)
    lag = 2 if n < chunks else 1
    own = [[cut(lane, at, ROWS) for at in starts] for lane in lanes]
    place = jnp.array([order.index(s) for s in range(n)], jnp.int32)
    me = lax.axis_index("shadow")
    ahead = (place[me] - place[root]) % n
    hops = jnp.stack([ahead, (n - ahead) % n])
    ways = (
        [(order[i], order[(i + 1) % n]) for i in range(n)],
        [(order[(i + 1) % n], order[i]) for i in range(n)],
    )
    weight = res_weight[:, None]
    steps = chunks + (n - 2) * lag
    came, last = [], None
    for t in range(steps):
        mine = tuple(own[i][t] for i in range(2)) if t < chunks else None
        if t >= lag:
            got = came[t - lag]
            if t == lag + 1:
                got, hops, weight = join(got, hops, weight)
            elif t == steps * 2 // 7:
                got, cold = join(got, cold)
                pre = jnp.dot(cold, gate_up, preferred_element_type=jnp.float32)
                cold = jnp.dot(swiglu(pre, hidden_units), down, preferred_element_type=jnp.float32).astype(jnp.bfloat16)
            elif t == steps * 2 // 7 + 1:
                got, cold = join(got, cold)
                cold = lax.all_to_all(cold, ("ep", "shadow"), 0, 0, tiled=True)
            elif t == steps - 2:
                got, cold = join(got, cold)
                scale = sum(jnp.where(chosen[k], cold_weights[:, k : k + 1], 0.0) for k in range(fan_out))
                high = lax.reduce_precision(scale, 8, 7)
                low = (scale - high).astype(jnp.bfloat16)
                cold = (
                    jnp.dot(high.astype(jnp.bfloat16), cold, preferred_element_type=jnp.float32)
                    + jnp.dot(low, cold, preferred_element_type=jnp.float32)
                ).astype(jnp.bfloat16)
            got, _ = join(got, last)
            mine = tuple(jnp.where(me == root, m, g) for m, g in zip(mine, got)) if t < chunks else got
        mine = last = join(*mine)
        came.append(tuple(lax.ppermute(mine[i], "shadow", ways[i]) for i in range(2)))
    came, cold = join(came, cold)
    hot_out = hot_expert(n, lag, hops, res_rows, weight, gate_up, down, [c for pair in came for c in pair])
    return hot_out, cold


def solution(mesh):
    order = ring_order(mesh)
    rows = P(("parts", "ep", "shadow"), None)
    owners = P(("ep", "shadow"), None, None)
    in_specs = (P("parts"), rows, P(("parts", "ep", "shadow")), rows, rows, rows, owners, owners)
    return jax.shard_map(
        lambda *args: body(order, *args), mesh=mesh, in_specs=in_specs, out_specs=(rows, rows), check_vma=False
    )
```

```python
import functools

import jax
import jax.numpy as jnp
from jax import lax
from jax.experimental import pallas as pl
from jax.experimental.pallas import tpu as pltpu
from jax.sharding import PartitionSpec as P

ROWS = 96
BLOCKS = 2


def ring_order(mesh):
    n = mesh.shape["shadow"]
    axis = mesh.axis_names.index("shadow")
    index = [0] * mesh.devices.ndim
    spots = []
    for s in range(n):
        index[axis] = s
        spots.append(tuple(getattr(mesh.devices[tuple(index)], "coords", (s,))))
    varying = [a for a in range(len(spots[0])) if len({p[a] for p in spots}) > 1]
    if len(varying) == 2:
        sizes = [len({p[a] for p in spots}) for a in varying]
        if 2 in sizes:
            short = varying[sizes.index(2)]
            long = varying[1 - sizes.index(2)]
            low = min(p[short] for p in spots)
            one = sorted((s for s in range(n) if spots[s][short] == low), key=lambda s: spots[s][long])
            two = sorted((s for s in range(n) if spots[s][short] != low), key=lambda s: -spots[s][long])
            return one + two
    return list(range(n))


def swiglu(pre, hidden_units):
    return (jax.nn.silu(pre[:, :hidden_units]) * pre[:, hidden_units:]).astype(jnp.bfloat16)


def both_ways(n, chunks, lag):
    return min(chunks, (n - 1 - n // 2) * lag // 2)


def order_of(n, chunks, lag):
    single = chunks - both_ways(n, chunks, lag)
    shared = [(lane, c) for c in range(single, chunks) for lane in range(2)]
    return [[(way, c) for c in range(single)] + shared for way in range(2)]


def arrivals(n, chunks, lag, h):
    single = chunks - both_ways(n, chunks, lag)
    nearer = 0 if h <= n // 2 else 1
    for way, turns in enumerate(order_of(n, chunks, lag)):
        for turn, (lane, c) in enumerate(turns):
            if c < single or way == nearer:
                yield lane, c, way, turn + lag * ((h, n - h)[way] - 1)


def hot_kernel(n, lag, hops, x, weight, gate_up, down, *rest):
    came = rest[:-5]
    out, gate_all, down_all, gate_sems, down_sem = rest[-5:]
    middle, half = gate_all.shape[0] // 2, down_all.shape[1] // 2
    rows = came[0].shape[0]
    starts = starts_of(middle + down_all.shape[0], rows)
    first = pl.program_id(0) == 0

    @pl.when(first)
    def _():
        @pl.when(hops[0] == 0)
        def _():
            for way in range(2):
                part = pl.ds(way * middle, middle)
                pltpu.make_async_copy(gate_up.at[part, :], gate_all.at[part, :], gate_sems.at[way]).start()
            pltpu.make_async_copy(down, down_all, down_sem).start()

        for h in range(1, n):

            @pl.when(hops[0] == h)
            def _(h=h):
                for lane, c, way, t in arrivals(n, len(starts), lag, h):
                    source = came[2 * t + way]
                    at = starts[c]
                    low = c * rows - at
                    gate = min(max(middle - at, low), rows)
                    if low < gate:
                        target = gate_all.at[pl.ds(lane * middle + at + low, gate - low), :]
                        part = source.at[pl.ds(low, gate - low), :]
                        pltpu.make_async_copy(part, target, gate_sems.at[lane]).start()
                    low = max(low, gate)
                    if low < rows:
                        target = down_all.at[pl.ds(at + low - middle, rows - low), pl.ds(lane * half, half)]
                        pltpu.make_async_copy(source.at[pl.ds(low, rows - low), :], target, down_sem).start()

    pre = 0.0
    for way in range(2):
        part = pl.ds(way * middle, middle)

        @pl.when(first)
        def _(way=way, part=part):
            pltpu.make_async_copy(gate_all.at[part, :], gate_all.at[part, :], gate_sems.at[way]).wait()

        pre += jnp.dot(x[:, part], gate_all[part, :], preferred_element_type=jnp.float32)
    hidden = swiglu(pre, down_all.shape[0])

    @pl.when(first)
    def _():
        pltpu.make_async_copy(down_all, down_all, down_sem).wait()

    total = jnp.dot(hidden, down_all[...], preferred_element_type=jnp.float32)
    out[...] = (total * weight[...]).astype(out.dtype)


def hot_expert(n, lag, hops, x, weight, gate_up, down, came):
    tokens, width = x.shape
    block = tokens // BLOCKS
    whole = pl.BlockSpec(memory_space=pl.ANY)
    return pl.pallas_call(
        functools.partial(hot_kernel, n, lag),
        grid=(BLOCKS,),
        out_shape=jax.ShapeDtypeStruct((tokens, width), jnp.bfloat16),
        in_specs=[
            pl.BlockSpec(memory_space=pltpu.SMEM),
            pl.BlockSpec((block, width), lambda i: (i, 0)),
            pl.BlockSpec((block, 1), lambda i: (i, 0)),
            whole,
            whole,
            *[whole for _ in came],
        ],
        out_specs=pl.BlockSpec((block, width), lambda i: (i, 0)),
        scratch_shapes=[
            pltpu.VMEM(gate_up.shape, gate_up.dtype),
            pltpu.VMEM(down.shape, down.dtype),
            pltpu.SemaphoreType.DMA((2,)),
            pltpu.SemaphoreType.DMA,
        ],
        compiler_params=pltpu.CompilerParams(vmem_limit_bytes=60 * 2**20),
        cost_estimate=pl.CostEstimate(
            flops=2 * tokens * (gate_up.size + down.size), bytes_accessed=20 * 2**20, transcendentals=0
        ),
    )(hops, x, weight, gate_up, down, *came)


def starts_of(total, rows):
    return [min(at, total - rows) for at in range(0, total, rows)]


def cut(parts, start, size):
    out = []
    for part in parts:
        low, high = max(start, 0), min(start + size, part.shape[0])
        if low < high:
            out.append(part[low:high])
        start -= part.shape[0]
    return out[0] if len(out) == 1 else jnp.concatenate(out, 0)


def join(*values):
    return lax.optimization_barrier(values)


def body(order, hot_root, res_rows, res_weight, cold_rows, cold_experts, cold_weights, w_gate_up, w_down):
    gate_up, down = w_gate_up[0], w_down[0]
    hidden_units, width = down.shape
    n = len(order)
    n_owners = lax.axis_size("ep") * n
    per_device, fan_out = cold_experts.shape
    capacity = max(2, 2 * per_device * fan_out // n_owners)

    slot = lax.broadcasted_iota(jnp.int32, (per_device, n_owners * capacity), 1)
    named = [cold_experts[:, k : k + 1] == slot // capacity for k in range(fan_out)]
    count = sum(m.astype(jnp.bfloat16) for m in named)
    before = (
        lax.broadcasted_iota(jnp.int32, (per_device, per_device), 0)
        > lax.broadcasted_iota(jnp.int32, (per_device, per_device), 1)
    ).astype(jnp.bfloat16)
    rank = jnp.dot(before, count, preferred_element_type=jnp.float32)
    here = rank == (slot % capacity).astype(jnp.float32)
    chosen = [m & here for m in named]
    placed = sum(m.astype(jnp.bfloat16) for m in chosen)
    outgoing = lax.dot_general(
        placed, cold_rows, (((0,), (0,)), ((), ())), preferred_element_type=jnp.float32
    ).astype(jnp.bfloat16)
    cold = lax.all_to_all(outgoing, ("ep", "shadow"), 0, 0, tiled=True)

    root = hot_root[lax.axis_index("ep")]
    half, middle = width // 2, gate_up.shape[0] // 2
    lanes = ([gate_up[:middle], down[:, :half]], [gate_up[middle:], down[:, half:]])
    starts = starts_of(middle + hidden_units, ROWS)
    chunks = len(starts)
    lag = 2 if n < chunks else 1
    own = [[cut(lane, at, ROWS) for at in starts] for lane in lanes]
    place = jnp.array([order.index(s) for s in range(n)], jnp.int32)
    me = lax.axis_index("shadow")
    ahead = (place[me] - place[root]) % n
    hops = jnp.stack([ahead, (n - ahead) % n])
    ways = (
        [(order[i], order[(i + 1) % n]) for i in range(n)],
        [(order[(i + 1) % n], order[i]) for i in range(n)],
    )
    weight = res_weight[:, None]
    turns = order_of(n, chunks, lag)
    sends = len(turns[0])
    steps = 1 + max(t for h in range(1, n) for _, _, _, t in arrivals(n, chunks, lag, h))
    came, last = [], None
    for t in range(steps):
        mine = tuple(own[lane][c] for lane, c in (turns[0][t], turns[1][t])) if t < sends else None
        if t >= lag:
            got = came[t - lag]
            if t == lag + 1:
                got, hops, weight = join(got, hops, weight)
            elif t == steps // 3:
                got, cold = join(got, cold)
                pre = jnp.dot(cold, gate_up, preferred_element_type=jnp.float32)
                cold = jnp.dot(swiglu(pre, hidden_units), down, preferred_element_type=jnp.float32).astype(jnp.bfloat16)
            elif t == steps // 3 + 1:
                got, cold = join(got, cold)
                cold = lax.all_to_all(cold, ("ep", "shadow"), 0, 0, tiled=True)
            elif t == steps - 2:
                got, cold = join(got, cold)
                scale = sum(jnp.where(chosen[k], cold_weights[:, k : k + 1], 0.0) for k in range(fan_out))
                high = lax.reduce_precision(scale, 8, 7)
                low = (scale - high).astype(jnp.bfloat16)
                cold = (
                    jnp.dot(high.astype(jnp.bfloat16), cold, preferred_element_type=jnp.float32)
                    + jnp.dot(low, cold, preferred_element_type=jnp.float32)
                ).astype(jnp.bfloat16)
            got, _ = join(got, last)
            mine = tuple(jnp.where(me == root, m, g) for m, g in zip(mine, got)) if t < sends else got
        mine = last = join(*mine)
        came.append(tuple(lax.ppermute(mine[i], "shadow", ways[i]) for i in range(2)))
    came, cold = join(came, cold)
    hot_out = hot_expert(n, lag, hops, res_rows, weight, gate_up, down, [c for pair in came for c in pair])
    return hot_out, cold


def solution(mesh):
    order = ring_order(mesh)
    rows = P(("parts", "ep", "shadow"), None)
    owners = P(("ep", "shadow"), None, None)
    in_specs = (P("parts"), rows, P(("parts", "ep", "shadow")), rows, rows, rows, owners, owners)
    return jax.shard_map(
        lambda *args: body(order, *args), mesh=mesh, in_specs=in_specs, out_specs=(rows, rows), check_vma=False
    )
```

```python
import functools

import jax
import jax.numpy as jnp
from jax import lax
from jax.experimental import pallas as pl
from jax.experimental.pallas import tpu as pltpu
from jax.sharding import PartitionSpec as P

ROWS = 96
BLOCKS = 2


def ring_order(mesh):
    n = mesh.shape["shadow"]
    axis = mesh.axis_names.index("shadow")
    index = [0] * mesh.devices.ndim
    spots = []
    for s in range(n):
        index[axis] = s
        spots.append(tuple(getattr(mesh.devices[tuple(index)], "coords", (s,))))
    varying = [a for a in range(len(spots[0])) if len({p[a] for p in spots}) > 1]
    if len(varying) == 2:
        sizes = [len({p[a] for p in spots}) for a in varying]
        if 2 in sizes:
            short = varying[sizes.index(2)]
            long = varying[1 - sizes.index(2)]
            low = min(p[short] for p in spots)
            one = sorted((s for s in range(n) if spots[s][short] == low), key=lambda s: spots[s][long])
            two = sorted((s for s in range(n) if spots[s][short] != low), key=lambda s: -spots[s][long])
            return one + two
    return list(range(n))


def swiglu(pre, hidden_units):
    return (jax.nn.silu(pre[:, :hidden_units]) * pre[:, hidden_units:]).astype(jnp.bfloat16)


def plan(n, chunks, lag):
    most = (n - 2) * lag
    single = chunks - most // 2
    ways = [[(way, c) for c in range(single)] + [None] * most for way in range(2)]
    meets = {}
    shared = [(lane, c) for c in range(single, chunks) for lane in range(2)]
    for k in range(1, n - 1):
        for i in range(lag):
            turns = (single + (n - 2 - k) * lag + i, single + (k - 1) * lag + i)
            chunk = shared[min(len(meets), len(shared) - 1)]
            meets.setdefault(chunk, (k, turns))
            for way in range(2):
                ways[way][turns[way]] = chunk
    return single, ways, meets


def arrivals(n, chunks, lag, h):
    single, _, meets = plan(n, chunks, lag)
    for way in range(2):
        for c in range(single):
            yield way, c, way, c + lag * ((h, n - h)[way] - 1)
    for (lane, c), (k, turns) in meets.items():
        way = 0 if h <= k else 1
        yield lane, c, way, turns[way] + lag * ((h, n - h)[way] - 1)


def hot_kernel(n, lag, hops, x, weight, gate_up, down, *rest):
    came = rest[:-5]
    out, gate_all, down_all, gate_sems, down_sem = rest[-5:]
    middle, half = gate_all.shape[0] // 2, down_all.shape[1] // 2
    rows = came[0].shape[0]
    starts = starts_of(middle + down_all.shape[0], rows)
    first = pl.program_id(0) == 0

    @pl.when(first)
    def _():
        @pl.when(hops[0] == 0)
        def _():
            for way in range(2):
                part = pl.ds(way * middle, middle)
                pltpu.make_async_copy(gate_up.at[part, :], gate_all.at[part, :], gate_sems.at[way]).start()
            pltpu.make_async_copy(down, down_all, down_sem).start()

        for h in range(1, n):

            @pl.when(hops[0] == h)
            def _(h=h):
                for lane, c, way, t in arrivals(n, len(starts), lag, h):
                    source = came[2 * t + way]
                    at = starts[c]
                    low = c * rows - at
                    gate = min(max(middle - at, low), rows)
                    if low < gate:
                        target = gate_all.at[pl.ds(lane * middle + at + low, gate - low), :]
                        part = source.at[pl.ds(low, gate - low), :]
                        pltpu.make_async_copy(part, target, gate_sems.at[lane]).start()
                    low = max(low, gate)
                    if low < rows:
                        target = down_all.at[pl.ds(at + low - middle, rows - low), pl.ds(lane * half, half)]
                        pltpu.make_async_copy(source.at[pl.ds(low, rows - low), :], target, down_sem).start()

    pre = 0.0
    for way in range(2):
        part = pl.ds(way * middle, middle)

        @pl.when(first)
        def _(way=way, part=part):
            pltpu.make_async_copy(gate_all.at[part, :], gate_all.at[part, :], gate_sems.at[way]).wait()

        pre += jnp.dot(x[:, part], gate_all[part, :], preferred_element_type=jnp.float32)
    hidden = swiglu(pre, down_all.shape[0])

    @pl.when(first)
    def _():
        pltpu.make_async_copy(down_all, down_all, down_sem).wait()

    total = jnp.dot(hidden, down_all[...], preferred_element_type=jnp.float32)
    out[...] = (total * weight[...]).astype(out.dtype)


def hot_expert(n, lag, hops, x, weight, gate_up, down, came):
    tokens, width = x.shape
    block = tokens // BLOCKS
    whole = pl.BlockSpec(memory_space=pl.ANY)
    return pl.pallas_call(
        functools.partial(hot_kernel, n, lag),
        grid=(BLOCKS,),
        out_shape=jax.ShapeDtypeStruct((tokens, width), jnp.bfloat16),
        in_specs=[
            pl.BlockSpec(memory_space=pltpu.SMEM),
            pl.BlockSpec((block, width), lambda i: (i, 0)),
            pl.BlockSpec((block, 1), lambda i: (i, 0)),
            whole,
            whole,
            *[whole for _ in came],
        ],
        out_specs=pl.BlockSpec((block, width), lambda i: (i, 0)),
        scratch_shapes=[
            pltpu.VMEM(gate_up.shape, gate_up.dtype),
            pltpu.VMEM(down.shape, down.dtype),
            pltpu.SemaphoreType.DMA((2,)),
            pltpu.SemaphoreType.DMA,
        ],
        compiler_params=pltpu.CompilerParams(vmem_limit_bytes=60 * 2**20),
        cost_estimate=pl.CostEstimate(
            flops=2 * tokens * (gate_up.size + down.size), bytes_accessed=20 * 2**20, transcendentals=0
        ),
    )(hops, x, weight, gate_up, down, *came)


def starts_of(total, rows):
    return [min(at, total - rows) for at in range(0, total, rows)]


def cut(parts, start, size):
    out = []
    for part in parts:
        low, high = max(start, 0), min(start + size, part.shape[0])
        if low < high:
            out.append(part[low:high])
        start -= part.shape[0]
    return out[0] if len(out) == 1 else jnp.concatenate(out, 0)


def join(*values):
    return lax.optimization_barrier(values)


def body(order, hot_root, res_rows, res_weight, cold_rows, cold_experts, cold_weights, w_gate_up, w_down):
    gate_up, down = w_gate_up[0], w_down[0]
    hidden_units, width = down.shape
    n = len(order)
    n_owners = lax.axis_size("ep") * n
    per_device, fan_out = cold_experts.shape
    capacity = max(2, 2 * per_device * fan_out // n_owners)

    slot = lax.broadcasted_iota(jnp.int32, (per_device, n_owners * capacity), 1)
    named = [cold_experts[:, k : k + 1] == slot // capacity for k in range(fan_out)]
    count = sum(m.astype(jnp.bfloat16) for m in named)
    before = (
        lax.broadcasted_iota(jnp.int32, (per_device, per_device), 0)
        > lax.broadcasted_iota(jnp.int32, (per_device, per_device), 1)
    ).astype(jnp.bfloat16)
    rank = jnp.dot(before, count, preferred_element_type=jnp.float32)
    here = rank == (slot % capacity).astype(jnp.float32)
    chosen = [m & here for m in named]
    placed = sum(m.astype(jnp.bfloat16) for m in chosen)
    outgoing = lax.dot_general(
        placed, cold_rows, (((0,), (0,)), ((), ())), preferred_element_type=jnp.float32
    ).astype(jnp.bfloat16)
    cold = lax.all_to_all(outgoing, ("ep", "shadow"), 0, 0, tiled=True)

    root = hot_root[lax.axis_index("ep")]
    half, middle = width // 2, gate_up.shape[0] // 2
    lanes = ([gate_up[:middle], down[:, :half]], [gate_up[middle:], down[:, half:]])
    starts = starts_of(middle + hidden_units, ROWS)
    chunks = len(starts)
    lag = 2 if n < chunks else 1
    own = [[cut(lane, at, ROWS) for at in starts] for lane in lanes]
    place = jnp.array([order.index(s) for s in range(n)], jnp.int32)
    me = lax.axis_index("shadow")
    ahead = (place[me] - place[root]) % n
    hops = jnp.stack([ahead, (n - ahead) % n])
    ways = (
        [(order[i], order[(i + 1) % n]) for i in range(n)],
        [(order[(i + 1) % n], order[i]) for i in range(n)],
    )
    weight = res_weight[:, None]
    _, turns, _ = plan(n, chunks, lag)
    sends = len(turns[0])
    steps = 1 + max(t for h in range(1, n) for _, _, _, t in arrivals(n, chunks, lag, h))
    came, last = [], None
    for t in range(steps):
        mine = tuple(own[lane][c] for lane, c in (turns[0][t], turns[1][t])) if t < sends else None
        if t >= lag:
            got = came[t - lag]
            if t == lag + 1:
                got, hops, weight = join(got, hops, weight)
            elif t == steps * 3 // 8:
                got, cold = join(got, cold)
                pre = jnp.dot(cold, gate_up, preferred_element_type=jnp.float32)
                cold = jnp.dot(swiglu(pre, hidden_units), down, preferred_element_type=jnp.float32).astype(jnp.bfloat16)
            elif t == steps * 3 // 8 + 1:
                got, cold = join(got, cold)
                cold = lax.all_to_all(cold, ("ep", "shadow"), 0, 0, tiled=True)
            elif t == steps - 2:
                got, cold = join(got, cold)
                scale = sum(jnp.where(chosen[k], cold_weights[:, k : k + 1], 0.0) for k in range(fan_out))
                high = lax.reduce_precision(scale, 8, 7)
                low = (scale - high).astype(jnp.bfloat16)
                cold = (
                    jnp.dot(high.astype(jnp.bfloat16), cold, preferred_element_type=jnp.float32)
                    + jnp.dot(low, cold, preferred_element_type=jnp.float32)
                ).astype(jnp.bfloat16)
            got, _ = join(got, last)
            mine = tuple(jnp.where(me == root, m, g) for m, g in zip(mine, got)) if t < sends else got
        mine = last = join(*mine)
        came.append(tuple(lax.ppermute(mine[i], "shadow", ways[i]) for i in range(2)))
    came, cold = join(came, cold)
    hot_out = hot_expert(n, lag, hops, res_rows, weight, gate_up, down, [c for pair in came for c in pair])
    return hot_out, cold


def solution(mesh):
    order = ring_order(mesh)
    rows = P(("parts", "ep", "shadow"), None)
    owners = P(("ep", "shadow"), None, None)
    in_specs = (P("parts"), rows, P(("parts", "ep", "shadow")), rows, rows, rows, owners, owners)
    return jax.shard_map(
        lambda *args: body(order, *args), mesh=mesh, in_specs=in_specs, out_specs=(rows, rows), check_vma=False
    )
```
